32 devices in a mesh: groups: 2 (over y), clusters: 16 (over z, x, core).
Axes of the slice: x: 2, y: 2, z: 4, core: 2. Of those that a mesh axis runs over, the one named last changes fastest.
Arguments:
- right_side: float32 [64, 512, 128], P(('groups', 'clusters')), parts along dimension 0, may hold values from -6 to 6
- diag_shift: float32 [64, 512], P(('groups', 'clusters')), parts along dimension 0, may hold values from 10 to 20
- self_blocks: bfloat16 [64, 512, 512], P(('groups', 'clusters')), parts along dimension 0, may hold values from -0.049804688 to 0.049804688
- near_blocks: bfloat16 [64, 512, 2048], P(('groups', 'clusters')), parts along dimension 0, may hold values from -0.019897461 to 0.019897461
- near_offset: int32 [256], P(('groups', 'clusters')), parts along dimension 0, may hold values from -2 to 2
- near_column: int32 [256], P(('groups', 'clusters')), parts along dimension 0, may hold values from 0 to 1
- far_factors: bfloat16 [64, 512, 2048], P(('groups', 'clusters')), parts along dimension 0, may hold values from -0.049804688 to 0.049804688
- far_peer: int32 [4096, 1], P(('groups', 'clusters')), parts along dimension 0, may hold values from 0 to 15; in each aligned block of 128 rows (0 to 127, 128 to 255, ...) at most 8 rows name the same one
Outputs:
- solution_field: float32 [64, 512, 128], P(('groups', 'clusters')), parts along dimension 0
- residual: float32 [64, 512, 128], P(('groups', 'clusters')), parts along dimension 0
The draws below stay inside these ranges and needn't reach their ends.
There are 2 independent parts, one for each index of `groups`. The reference program is written for one: setup_inputs(seed, part) draws one part's arguments, and reference() takes and returns one part's arrays. A program takes and returns all parts, laid end to end along the dimension named above; each array names one. Nothing has to cross between parts.
Inputs may be any that keep to these rules, and one draw needn't show every extreme that they name: `far_peer`: in the rows of one device no device is named more than 8 times, and some device is named exactly 8 times in some device's rows.
All inputs are finite; a program needn't handle non-finite values.
Results may differ from the reference program's by a relative error of at most 0.0003.
Values may be sent and summed in bfloat16 or wider, within the bound.
A program may use at most 128 MiB of HBM per device.

```python
import math
import jax
import jax.numpy as jnp
import numpy as np
from jax import lax

PAN = 512
MODES = 128
RANK = 32
CL_DEV = 2
NEAR_CL = 4
FAR_CL = 64
REACH = 2
ITERS = 2
CLUSTERS = 32
FAR_DEV = 128
CAP = 8
N_CLUSTERS = 16


def plant(array, own_key, least, largest):
    spot = [jax.random.randint(jax.random.fold_in(own_key, axis), (), 0, length) for axis, length in enumerate(array.shape)]
    longest = array.shape.index(max(array.shape))
    neighbour = spot[:longest] + [(spot[longest] + 1) % array.shape[longest]] + spot[longest + 1:]
    return array.at[tuple(spot)].set(least).at[tuple(neighbour)].set(largest)


def steps_of(stream_key, dims, pieces, low, largest):
    loudness = 1.0
    for axis_at, parts in pieces:
        draws = jax.random.uniform(jax.random.fold_in(jax.random.fold_in(stream_key, 6), axis_at), (parts,), jnp.float32, low / len(pieces), largest / len(pieces))
        loudness = loudness * jnp.repeat(jnp.exp(draws), dims[axis_at] // parts).reshape((-1,) + (1,) * (len(dims) - 1 - axis_at))
    return loudness


def deal_out(stream_key, own, number, rows, amount, top, limit, lean):
    order = jax.random.permutation(stream_key, amount)
    heavy_load, usual = shares(amount, rows * top, limit, lean, True), shares(amount, rows * top, limit, lean, False)
    places = jnp.arange(amount)

    def named(tallies, turn):
        used = int((tallies > 0).sum())
        fixed = max(1, used // 4)
        passed = fixed + (places - fixed + turn * (used - fixed)) % max(1, amount - fixed)
        return jnp.zeros((amount,), jnp.int32).at[order[jnp.where(places < fixed, places, passed)]].set(jnp.asarray(tallies, jnp.int32))

    tallies = jnp.where(number % 4 == 0, named(heavy_load, number // 4), named(usual, number - number // 4 - 1))
    mixed = jax.random.permutation(jax.random.fold_in(own, 3), amount)
    giver, receiver = mixed[0:amount // 2 * 2:2], mixed[1:amount // 2 * 2:2]
    room = jnp.minimum(tallies[giver] - 1, limit - tallies[receiver]) // 2
    room = jnp.where((giver == order[0]) | (receiver == order[0]) | (tallies[receiver] == 0), 0, jnp.maximum(room, 0))
    passed = jax.random.randint(jax.random.fold_in(own, 4), (amount // 2,), 0, 1 << 20) % (room + 1)
    tallies = tallies.at[giver].add(-passed).at[receiver].add(passed)
    members = jnp.searchsorted(jnp.cumsum(tallies), jnp.arange(rows * top), side="right").astype(jnp.int32)
    grid = members.reshape(top, rows).T
    grid = grid[jax.random.permutation(jax.random.fold_in(own, 1), rows)]
    turn = jax.random.randint(jax.random.fold_in(own, 2), (rows, 1), 0, top)
    return jnp.take_along_axis(grid, (jnp.arange(top)[None, :] + turn) % top, axis=1)


def shares(amount, total, most, slope, full):
    loads = [(1 << 20) // math.isqrt(standing ** slope) + 1 for standing in range(1, amount + 1)]
    largest = most if full else min(most, max(-(-total // amount), total * loads[0] // sum(loads)))
    least = 1 if total - largest >= amount - 1 else 0
    counts, spare = [largest] + [least] * (amount - 1), total - largest - least * (amount - 1)
    while spare > 0:
        movable = [i for i in range(1, amount) if counts[i] < largest] or [i for i in range(1, amount) if counts[i] < most]
        pool, remaining = sum([loads[i] for i in movable]), spare
        for i in movable:
            addition = min(most - counts[i], max(1, remaining * loads[i] // pool), spare)
            counts[i] = counts[i] + addition
            spare = spare - addition
    return np.array(counts)


def scatter_about(key, dims, spread, bound, cuts=(), kind=jnp.bfloat16):
    level = steps_of(key, dims, cuts, -0.22, 0.18) if cuts else 1.0
    drawn = jax.random.normal(key, dims, jnp.float32) * spread * level
    return jnp.minimum(jnp.maximum(drawn, -bound), bound).astype(kind)


def setup_inputs(seed: int = 0, part: int = 0) -> dict:
    key_of = jax.random.split(jax.random.key(seed), 9)
    part_keys = jax.random.split(jax.random.fold_in(key_of[8], part), 9)
    right_side = scatter_about(part_keys[0], (CLUSTERS, PAN, MODES), 1.0, 6.0, ((0, 16),), jnp.float32)
    diag_shift = jnp.clip(jnp.exp(math.log(20.0) - 0.6931472 * jax.random.uniform(part_keys[1], (CLUSTERS, PAN), jnp.float32) ** steps_of(part_keys[1], (CLUSTERS, PAN), ((0, 16),), -0.2, 0.2)), 10.0, 20.0)
    self_blocks = jnp.clip(jax.random.uniform(part_keys[2], (CLUSTERS, PAN, PAN), jnp.float32, -0.049804688, 0.049804688) * steps_of(part_keys[2], (CLUSTERS, PAN, PAN), ((0, 16),), -0.4, 0.0), -0.049804688, 0.049804688).astype(jnp.bfloat16)
    near_blocks = jnp.clip(jax.random.uniform(part_keys[3], (CLUSTERS, PAN, NEAR_CL * PAN), jnp.float32, -0.019897461, 0.019897461) * steps_of(part_keys[3], (CLUSTERS, PAN, NEAR_CL * PAN), ((0, 16),), -0.4, 0.0), -0.019897461, 0.019897461).astype(jnp.bfloat16)
    near_offset = plant(jax.random.randint(part_keys[4], (CLUSTERS * NEAR_CL,), 0 - REACH, REACH + 1), jax.random.fold_in(part_keys[4], 1), 0 - REACH, REACH).astype(jnp.int32)
    near_column = plant(jax.random.randint(part_keys[5], (CLUSTERS * NEAR_CL,), 0, CL_DEV), jax.random.fold_in(part_keys[5], 1), 0, CL_DEV - 1).astype(jnp.int32)
    far_factors = jnp.clip(jax.random.uniform(part_keys[6], (CLUSTERS, PAN, FAR_CL * RANK), jnp.float32, -0.049804688, 0.049804688) * steps_of(part_keys[6], (CLUSTERS, PAN, FAR_CL * RANK), ((0, 16),), -0.4, 0.0), -0.049804688, 0.049804688).astype(jnp.bfloat16)
    far_peer_keys = jax.random.split(jax.random.fold_in(part_keys[7], 1), (CLUSTERS * FAR_CL) // FAR_DEV)
    far_peer_turns = jax.random.permutation(jax.random.fold_in(part_keys[7], 3), (CLUSTERS * FAR_CL) // FAR_DEV)
    far_peer = jax.vmap(lambda own, number: deal_out(jax.random.fold_in(part_keys[7], 2), own, number, FAR_DEV, N_CLUSTERS, 1, CAP, 2))(far_peer_keys, far_peer_turns).reshape((CLUSTERS * FAR_CL, 1))
    return {"right_side": right_side, "diag_shift": diag_shift, "self_blocks": self_blocks, "near_blocks": near_blocks, "near_offset": near_offset, "near_column": near_column, "far_factors": far_factors, "far_peer": far_peer}


def spd_solve(matrix, target):
    lower = jnp.linalg.cholesky(matrix)
    middle = lax.linalg.triangular_solve(lower, target, left_side=True, lower=True)
    return lax.linalg.triangular_solve(lower, middle, left_side=True, lower=True, transpose_a=True)

def gram(left, right):
    return jnp.dot(left.reshape(-1, MODES).T, right.reshape(-1, MODES), precision=lax.Precision.HIGHEST)

def combine(block, coeff):
    return jnp.dot(block.reshape(-1, MODES), coeff, precision=lax.Precision.HIGHEST).reshape(block.shape)

def near_terms(packed, near_blocks, near_offset, near_column):
    pair_index = jnp.arange(CLUSTERS * NEAR_CL, dtype=jnp.int32)
    device_of = pair_index // (CL_DEV * NEAR_CL)
    target = device_of + near_offset
    live = (target >= 0) & (target < N_CLUSTERS)
    partner = (jnp.clip(target, 0, N_CLUSTERS - 1) * CL_DEV + near_column).astype(jnp.int32)
    partner = partner.reshape(CLUSTERS, NEAR_CL)
    live_mask = live.astype(jnp.float32).reshape(CLUSTERS, NEAR_CL)

    def visit(total, inputs):
        block, own, friends, alive = inputs
        fetched = packed[friends] * alive[:, None, None].astype(jnp.bfloat16)
        forward = jnp.dot(block.astype(jnp.float32), fetched.reshape(NEAR_CL * PAN, MODES).astype(jnp.float32), preferred_element_type=jnp.float32)
        mirrored = jnp.dot(block.T.astype(jnp.float32), own.astype(jnp.float32), preferred_element_type=jnp.float32).reshape(NEAR_CL, PAN, MODES)
        total = total.at[friends].add(mirrored * alive[:, None, None])
        return (total, forward)
    start = jnp.zeros((CLUSTERS, PAN, MODES), jnp.float32)
    total, forward = lax.scan(visit, start, (near_blocks, packed, partner, live_mask))
    return total + forward

def far_terms(packed, far_factors, far_peer):
    halves = CLUSTERS * FAR_CL
    compressed = lax.map(lambda pair: jnp.dot(pair[0].T.astype(jnp.float32), pair[1].astype(jnp.float32), preferred_element_type=jnp.float32).astype(jnp.bfloat16), (far_factors, packed))
    compressed = compressed.reshape(halves, RANK, MODES)
    peers = far_peer[:, 0].reshape(N_CLUSTERS, FAR_DEV)
    peer_hot = (peers[:, :, None] == jnp.arange(N_CLUSTERS, dtype=jnp.int32)[None, None, :]).astype(jnp.int32)
    earlier = jnp.cumsum(peer_hot, axis=1) - peer_hot
    ranking = jnp.sum(earlier * peer_hot, axis=2)
    device_ids = jnp.arange(N_CLUSTERS, dtype=jnp.int32)[:, None]
    code_out = ((device_ids * N_CLUSTERS + peers) * CAP + ranking).reshape(-1).astype(jnp.int32)
    code_in = ((peers * N_CLUSTERS + device_ids) * CAP + ranking).reshape(-1).astype(jnp.int32)
    table = jnp.full((N_CLUSTERS * N_CLUSTERS * CAP,), -1, jnp.int32).at[code_out].set(jnp.arange(halves, dtype=jnp.int32))
    partner = table[code_in]
    matched = jnp.where((partner >= 0)[:, None, None], compressed[jnp.maximum(partner, 0)], jnp.zeros_like(compressed))
    matched = matched.reshape(CLUSTERS, FAR_CL * RANK, MODES)
    return lax.map(lambda pair: jnp.dot(pair[0].astype(jnp.float32), pair[1].astype(jnp.float32), preferred_element_type=jnp.float32), (far_factors, matched))

def operate(direction, diag_shift, self_blocks, near_blocks, near_offset, near_column, far_factors, far_peer):
    packed = direction.astype(jnp.bfloat16)
    image = diag_shift[:, :, None] * direction
    image = image + lax.map(lambda pair: 0.5 * (jnp.dot(pair[0].astype(jnp.float32), pair[1].astype(jnp.float32), preferred_element_type=jnp.float32) + jnp.dot(pair[0].T.astype(jnp.float32), pair[1].astype(jnp.float32), preferred_element_type=jnp.float32)), (self_blocks, packed))
    image = image + near_terms(packed, near_blocks, near_offset, near_column)
    image = image + far_terms(packed, far_factors, far_peer)
    return image

def reference(right_side, diag_shift, self_blocks, near_blocks, near_offset, near_column, far_factors, far_peer):
    solution_field = jnp.zeros_like(right_side)
    residual = right_side
    direction = right_side
    current = gram(residual, residual)
    for step in range(ITERS):
        image = operate(direction, diag_shift, self_blocks, near_blocks, near_offset, near_column, far_factors, far_peer)
        step_size = spd_solve(gram(direction, image), current)
        solution_field = solution_field + combine(direction, step_size)
        residual = residual - combine(image, step_size)
        if step + 1 < ITERS:
            later = gram(residual, residual)
            blend = spd_solve(current, later)
            direction = residual + combine(direction, blend)
            current = later
    return (solution_field, residual)
```

```python
import functools

import jax
import jax.numpy as jnp
from jax import lax
from jax.experimental import pallas as pl
from jax.experimental.pallas import tpu as pltpu
from jax.sharding import PartitionSpec as P

MESH = pl.DeviceIdType.MESH
RANK = 32
REACH = 2
ITERS = 2
HIGH = lax.Precision.HIGHEST


def hdot(left, right, dims=((1,), (0,))):
    return lax.dot_general(left, right, (dims, ((), ())), precision=HIGH, preferred_element_type=jnp.float32)


def invert(mats):
    size = mats[0].shape[0]
    rows = lax.broadcasted_iota(jnp.int32, (size, size), 0)
    lanes = lax.broadcasted_iota(jnp.int32, (size, size), 1)

    def body(_, mats):
        done = []
        for a in mats:
            for k in range(8):
                column = a[:, k : k + 1]
                pivot = 1.0 / a[k : k + 1, k : k + 1]
                line = jnp.where(lanes[:1] == k, pivot, a[k : k + 1] * pivot)
                a = jnp.where(rows == k, line, jnp.where(lanes == k, 0.0, a) - column * line)
            a = pltpu.roll(a, size - 8, 1)
            done.append(jnp.concatenate([a[8:], a[:8]], axis=0))
        return tuple(done)

    return lax.fori_loop(0, size // 8, body, tuple(mats))


def meet(devices):
    me = lax.axis_index("clusters")
    barrier = pltpu.get_barrier_semaphore()

    def greet(k, carry):
        peer = lax.rem(me + k, devices)
        pl.semaphore_signal(barrier, inc=1, device_id={"clusters": peer}, device_id_type=MESH)
        return carry

    lax.fori_loop(1, devices, greet, 0)
    pl.semaphore_wait(barrier, devices - 1)


def reduce_all(devices, part, landing, total, sems):
    me = lax.axis_index("clusters")
    pieces = part.shape[0]
    send_a, recv_a, send_b, recv_b = sems

    def copy_a(k, peer):
        return pltpu.make_async_remote_copy(
            src_ref=part.at[peer], dst_ref=landing.at[k], send_sem=send_a.at[k], recv_sem=recv_a.at[k],
            device_id={"clusters": peer}, device_id_type=MESH)

    def copy_b(k, peer, piece):
        return pltpu.make_async_remote_copy(
            src_ref=total.at[piece], dst_ref=total.at[piece], send_sem=send_b.at[k], recv_sem=recv_b.at[k],
            device_id={"clusters": peer}, device_id_type=MESH)

    def loop(fn):
        def body(k, carry):
            fn(k)
            return carry
        lax.fori_loop(1, devices, body, 0)

    def send_one(k):
        peer = lax.rem(me + k, devices)
        if pieces == devices:
            copy_a(k, peer).start()
        else:
            @pl.when(peer < pieces)
            def _():
                copy_a(k, peer).start()

    loop(send_one)

    def gather():
        def add(k, acc):
            copy_a(k, 0).wait_recv()
            return acc + landing[k]
        total[me] = lax.fori_loop(1, devices, add, part[me])
        loop(lambda k: copy_b(k, lax.rem(me + k, devices), me).start())

    if pieces == devices:
        gather()
    else:
        pl.when(me < pieces)(gather)

    def arrive(k):
        origin = lax.rem(me - k + devices, devices)
        if pieces == devices:
            copy_b(k, 0, origin).wait_recv()
        else:
            @pl.when(origin < pieces)
            def _():
                copy_b(k, 0, origin).wait_recv()

    loop(arrive)

    def finish(k):
        peer = lax.rem(me + k, devices)
        if pieces == devices:
            copy_a(k, peer).wait_send()
            copy_b(k, peer, me).wait_send()
        else:
            @pl.when(peer < pieces)
            def _():
                copy_a(k, peer).wait_send()

            @pl.when(me < pieces)
            def _():
                copy_b(k, peer, me).wait_send()

    loop(finish)


def symmetric(mat):
    return 0.5 * (mat + mat.T)


def first_kernel(devices, part, step_ref, later_ref, blend_ref, landing, total, *sems):
    meet(devices)
    reduce_all(devices, part, landing, total, sems)
    modes = part.shape[-1]
    whole = total[...].reshape(-1, modes)
    current, curvature, squared = whole[:modes], whole[modes : 2 * modes], whole[2 * modes :]
    inv_curv, inv_cur = invert([symmetric(curvature), symmetric(current)])
    step = hdot(inv_curv, current)
    cross = hdot(curvature, step)
    later = current - cross - cross.T + hdot(step.T, hdot(squared, step))
    step_ref[...] = step
    later_ref[...] = later
    blend_ref[...] = hdot(inv_cur, later)


def last_kernel(devices, part, current, step_ref, landing, total, *sems):
    meet(devices)
    reduce_all(devices, part, landing, total, sems)
    (inv_curv,) = invert([symmetric(total[...].reshape(part.shape[-1], part.shape[-1]))])
    step_ref[...] = hdot(inv_curv, current[...])


def solve_call(kernel, grams, extra, outs, ident):
    devices = lax.axis_size("clusters")
    modes = grams.shape[-1]
    pieces = min(devices, grams.shape[0] // 8)
    part = grams.reshape(pieces, -1, modes)
    square = jax.ShapeDtypeStruct((modes, modes), jnp.float32)
    vmem = pl.BlockSpec(memory_space=pltpu.VMEM)
    return pl.pallas_call(
        functools.partial(kernel, devices),
        out_shape=[square] * outs,
        in_specs=[vmem] * (1 + len(extra)),
        out_specs=[vmem] * outs,
        scratch_shapes=[
            pltpu.VMEM((devices,) + part.shape[1:], jnp.float32),
            pltpu.VMEM(part.shape, jnp.float32),
        ] + [pltpu.SemaphoreType.DMA((devices,))] * 4,
        compiler_params=pltpu.CompilerParams(collective_id=ident, has_side_effects=True, vmem_limit_bytes=32 << 20),
    )(part, *extra)


def from_behind(value, axis, steps):
    count = lax.axis_size(axis)
    leading, last = (max(0, -steps), min(count, count - steps))
    return lax.ppermute(value, axis, [(source, source + steps) for source in range(leading, last)])


def local_gram(left, right):
    modes = left.shape[-1]
    return jnp.dot(
        left.reshape(-1, modes).T, right.reshape(-1, modes), precision=lax.Precision.HIGHEST
    )


def combine(block, coeff):
    modes = block.shape[-1]
    return jnp.dot(block.reshape(-1, modes), coeff, precision=lax.Precision.HIGHEST).reshape(
        block.shape
    )


def shards(
    right_side,
    diag_shift,
    self_blocks,
    near_blocks,
    near_offset,
    near_column,
    far_factors,
    far_peer,
):
    cl_dev, panels, modes = right_side.shape
    devices = lax.axis_size("clusters")
    far_dev = far_peer.shape[0]
    near_cl = near_blocks.shape[2] // panels
    capacity = max(2, -(-far_dev // devices))
    peers = far_peer[:, 0]
    peer_hot = (peers[:, None] == jnp.arange(devices, dtype=jnp.int32)[None, :]).astype(jnp.int32)
    earlier = jnp.cumsum(peer_hot, axis=0) - peer_hot
    ranking = jnp.sum(earlier * peer_hot, axis=1)
    slot_of = peers * capacity + ranking
    slot_table = (
        slot_of[None, :] == jnp.arange(devices * capacity, dtype=jnp.int32)[:, None]
    ).astype(jnp.bfloat16)
    span = 2 * REACH + 1
    window_pos = (near_offset + REACH) * cl_dev + near_column
    window_table = (
        window_pos[None, :] == jnp.arange(span * cl_dev, dtype=jnp.int32)[:, None]
    ).astype(jnp.float32)
    residual = right_side
    direction = right_side
    for step in range(ITERS):
        packed = direction.astype(jnp.bfloat16)
        image = diag_shift[:, :, None] * direction
        straight = jnp.einsum(
            "cpk,ckm->cpm", self_blocks, packed, preferred_element_type=jnp.float32
        )
        flipped = jnp.einsum(
            "ckp,ckm->cpm", self_blocks, packed, preferred_element_type=jnp.float32
        )
        image = image + 0.5 * (straight + flipped)
        slabs = []
        for offset in range(-REACH, REACH + 1):
            if offset == 0:
                slabs.append(packed)
            else:
                slabs.append(from_behind(packed, "clusters", -offset))
        window = jnp.concatenate(slabs, axis=0)
        fetched = jnp.take(window, window_pos, axis=0).reshape(cl_dev, near_cl * panels, modes)
        image = image + jnp.einsum(
            "cpk,ckm->cpm", near_blocks, fetched, preferred_element_type=jnp.float32
        )
        mirrored = jnp.einsum(
            "cpk,cpm->ckm", near_blocks, packed, preferred_element_type=jnp.float32
        )
        mirrored = mirrored.reshape(cl_dev * near_cl, panels * modes)
        returned = jnp.dot(window_table, mirrored, precision=lax.Precision.HIGHEST).reshape(
            span, cl_dev, panels, modes
        )
        image = image + returned[REACH]
        for offset in range(-REACH, REACH + 1):
            if offset != 0:
                image = image + from_behind(returned[offset + REACH], "clusters", offset)
        compressed = jnp.einsum(
            "cpk,cpm->ckm", far_factors, packed, preferred_element_type=jnp.float32
        ).astype(jnp.bfloat16)
        compressed = compressed.reshape(far_dev, RANK * modes)
        outgoing = jnp.dot(slot_table, compressed, preferred_element_type=jnp.float32).astype(
            jnp.bfloat16
        )
        outgoing = outgoing.reshape(devices, capacity, RANK * modes)
        incoming = lax.all_to_all(
            outgoing, "clusters", split_axis=0, concat_axis=0, tiled=True
        ).reshape(devices * capacity, RANK * modes)
        matched = jnp.dot(slot_table.T, incoming, preferred_element_type=jnp.float32).astype(
            jnp.bfloat16
        )
        matched = matched.reshape(cl_dev, far_dev // cl_dev * RANK, modes)
        image = image + jnp.einsum(
            "cpk,ckm->cpm", far_factors, matched, preferred_element_type=jnp.float32
        )
        if step == 0:
            grams = jnp.concatenate(
                [local_gram(residual, residual), local_gram(direction, image), local_gram(image, image)]
            )
            step_size, current, blend = solve_call(first_kernel, grams, (), 3, 1)
            solution_field = combine(direction, step_size)
            residual = residual - combine(image, step_size)
            direction = residual + combine(direction, blend)
        else:
            (step_size,) = solve_call(last_kernel, local_gram(direction, image), (current,), 1, 2)
            solution_field = solution_field + combine(direction, step_size)
            residual = residual - combine(image, step_size)
    return (solution_field, residual)


def solution(mesh):
    in_specs = (
        P(("groups", "clusters"), None, None),
        P(("groups", "clusters"), None),
        P(("groups", "clusters"), None, None),
        P(("groups", "clusters"), None, None),
        P(("groups", "clusters")),
        P(("groups", "clusters")),
        P(("groups", "clusters"), None, None),
        P(("groups", "clusters"), None),
    )
    out_specs = (P(("groups", "clusters"), None, None), P(("groups", "clusters"), None, None))
    return jax.shard_map(shards, mesh=mesh, in_specs=in_specs, out_specs=out_specs, check_vma=False)
```

```python
import functools

import jax
import jax.numpy as jnp
from jax import lax
from jax.experimental import pallas as pl
from jax.experimental.pallas import tpu as pltpu
from jax.sharding import PartitionSpec as P

MESH = pl.DeviceIdType.MESH
RANK = 32
REACH = 2
ITERS = 2
HIGH = lax.Precision.HIGHEST


def hdot(left, right, dims=((1,), (0,))):
    return lax.dot_general(left, right, (dims, ((), ())), precision=HIGH, preferred_element_type=jnp.float32)


def invert(mats):
    size = mats[0].shape[0]
    rows = lax.broadcasted_iota(jnp.int32, (size, size), 0)
    lanes = lax.broadcasted_iota(jnp.int32, (size, size), 1)

    def body(_, mats):
        done = []
        for a in mats:
            for k in range(8):
                column = a[:, k : k + 1]
                pivot = 1.0 / a[k : k + 1, k : k + 1]
                line = jnp.where(lanes[:1] == k, pivot, a[k : k + 1] * pivot)
                a = jnp.where(rows == k, line, jnp.where(lanes == k, 0.0, a) - column * line)
            a = pltpu.roll(a, size - 8, 1)
            done.append(jnp.concatenate([a[8:], a[:8]], axis=0))
        return tuple(done)

    return lax.fori_loop(0, size // 8, body, tuple(mats))


def meet(devices):
    me = lax.axis_index("clusters")
    barrier = pltpu.get_barrier_semaphore()

    def greet(k, carry):
        peer = lax.rem(me + k, devices)
        pl.semaphore_signal(barrier, inc=1, device_id={"clusters": peer}, device_id_type=MESH)
        return carry

    lax.fori_loop(1, devices, greet, 0)
    pl.semaphore_wait(barrier, devices - 1)


def reduce_all(devices, part, landing, total, sems):
    me = lax.axis_index("clusters")
    pieces = part.shape[0]
    send_a, recv_a, send_b, recv_b = sems

    def copy_a(k, peer):
        return pltpu.make_async_remote_copy(
            src_ref=part.at[peer], dst_ref=landing.at[k], send_sem=send_a.at[k], recv_sem=recv_a.at[k],
            device_id={"clusters": peer}, device_id_type=MESH)

    def copy_b(k, peer, piece):
        return pltpu.make_async_remote_copy(
            src_ref=total.at[piece], dst_ref=total.at[piece], send_sem=send_b.at[k], recv_sem=recv_b.at[k],
            device_id={"clusters": peer}, device_id_type=MESH)

    def loop(fn):
        def body(k, carry):
            fn(k)
            return carry
        lax.fori_loop(1, devices, body, 0)

    def send_one(k):
        peer = lax.rem(me + k, devices)
        if pieces == devices:
            copy_a(k, peer).start()
        else:
            @pl.when(peer < pieces)
            def _():
                copy_a(k, peer).start()

    loop(send_one)

    def gather():
        def add(k, acc):
            copy_a(k, 0).wait_recv()
            return acc + landing[k]
        total[me] = lax.fori_loop(1, devices, add, part[me])
        loop(lambda k: copy_b(k, lax.rem(me + k, devices), me).start())

    if pieces == devices:
        gather()
    else:
        pl.when(me < pieces)(gather)

    def arrive(k):
        origin = lax.rem(me - k + devices, devices)
        if pieces == devices:
            copy_b(k, 0, origin).wait_recv()
        else:
            @pl.when(origin < pieces)
            def _():
                copy_b(k, 0, origin).wait_recv()

    loop(arrive)

    def finish(k):
        peer = lax.rem(me + k, devices)
        if pieces == devices:
            copy_a(k, peer).wait_send()
            copy_b(k, peer, me).wait_send()
        else:
            @pl.when(peer < pieces)
            def _():
                copy_a(k, peer).wait_send()

            @pl.when(me < pieces)
            def _():
                copy_b(k, peer, me).wait_send()

    loop(finish)


def symmetric(mat):
    return 0.5 * (mat + mat.T)


def fast_dot(left, right):
    return jnp.dot(left, right, preferred_element_type=jnp.float32)


def times(count, fn):
    def body(k, carry):
        fn(k)
        return carry
    lax.fori_loop(0, count, body, 0)


def kernel(
    devices, right_ref, diag_ref, self_hbm, near_hbm, far_hbm, offset_ref, column_ref, peer_ref, rank_ref, source_ref,
    field_ref, resid_ref,
    own, near, far, direction, image, turned, window, window_sems, mirrored, returned, landed, mirror_sems,
    compressed, outgoing, incoming, far_send, far_recv, matched, part_a, landing_a, total_a, part_b, landing_b, total_b,
    load_sems, send_a, recv_a, send_b, recv_b,
):
    me = lax.axis_index("clusters")
    cl_dev, panels, modes = right_ref.shape
    near_cl = near.shape[2] // panels
    far_cl = far.shape[2] // RANK
    capacity = outgoing.shape[1]
    far_dev = cl_dev * far_cl
    offsets = [o for o in range(-REACH, REACH + 1) if o]
    sems = (send_a, recv_a, send_b, recv_b)

    loads = [
        pltpu.make_async_copy(far_hbm, far, load_sems.at[0]),
        pltpu.make_async_copy(near_hbm, near, load_sems.at[1]),
        pltpu.make_async_copy(self_hbm, own, load_sems.at[2]),
    ]
    for load in loads:
        load.start()

    def inside(offset):
        return (me + offset >= 0) & (me + offset < devices)

    for offset in offsets:
        @pl.when(jnp.logical_not(inside(offset)))
        def _():
            window[offset + REACH] = jnp.zeros(window.shape[1:], window.dtype)
    compressed[far_dev] = jnp.zeros(compressed.shape[1:], compressed.dtype)
    direction[...] = right_ref[...]
    resid_ref[...] = right_ref[...]
    meet(devices)

    def window_copy(offset):
        return pltpu.make_async_remote_copy(
            src_ref=window.at[REACH], dst_ref=window.at[REACH - offset],
            send_sem=window_sems.at[0, REACH + offset], recv_sem=window_sems.at[1, REACH - offset],
            device_id={"clusters": me + offset}, device_id_type=MESH)

    def window_from(offset):
        return pltpu.make_async_remote_copy(
            src_ref=window.at[REACH], dst_ref=window.at[REACH + offset],
            send_sem=window_sems.at[0, REACH + offset], recv_sem=window_sems.at[1, REACH + offset],
            device_id={"clusters": me + offset}, device_id_type=MESH)

    def mirror_copy(offset):
        return pltpu.make_async_remote_copy(
            src_ref=returned.at[REACH + offset], dst_ref=landed.at[REACH - offset],
            send_sem=mirror_sems.at[0, REACH + offset], recv_sem=mirror_sems.at[1, REACH - offset],
            device_id={"clusters": me + offset}, device_id_type=MESH)

    def mirror_from(offset):
        return pltpu.make_async_remote_copy(
            src_ref=returned.at[REACH + offset], dst_ref=landed.at[REACH + offset],
            send_sem=mirror_sems.at[0, REACH + offset], recv_sem=mirror_sems.at[1, REACH + offset],
            device_id={"clusters": me + offset}, device_id_type=MESH)

    def far_copy(k, peer, slot):
        return pltpu.make_async_remote_copy(
            src_ref=outgoing.at[peer], dst_ref=incoming.at[slot], send_sem=far_send.at[k], recv_sem=far_recv.at[k],
            device_id={"clusters": peer}, device_id_type=MESH)

    def when_inside(fn):
        for offset in offsets:
            @pl.when(inside(offset))
            def _():
                fn(offset)

    def operate(first):
        for c in range(cl_dev):
            value = direction[c]
            window[REACH, c] = value.astype(jnp.bfloat16)
            turned[c] = value.T.astype(jnp.bfloat16)
        when_inside(lambda o: window_copy(o).start())

        if first:
            loads[0].wait()
        tiles = far_cl * RANK // panels
        tile_halves = panels // RANK

        def compress(i):
            c, q = i // tiles, i % tiles
            columns = pl.ds(pl.multiple_of(q * panels, panels), panels)
            value = fast_dot(turned[c], far[c, :, columns]).T.astype(jnp.bfloat16)
            compressed[pl.ds(i * tile_halves, tile_halves)] = value.reshape(tile_halves, RANK, modes)

        times(cl_dev * tiles, compress)

        def post(k):
            peer = lax.rem(me + k, devices)
            for r in range(capacity):
                outgoing[peer, r] = compressed[source_ref[peer * capacity + r]]

        def send(k):
            post(k + 1)
            far_copy(k + 1, lax.rem(me + k + 1, devices), me).start()

        times(devices - 1, send)
        for r in range(capacity):
            incoming[me, r] = compressed[source_ref[me * capacity + r]]

        if first:
            loads[1].wait()

        def mirror(i):
            c, q = i // near_cl, i % near_cl
            columns = pl.ds(pl.multiple_of(q * panels, panels), panels)
            mirrored[i] = fast_dot(turned[c], near[c, :, columns]).T

        times(cl_dev * near_cl, mirror)

        for o in [1, -1, 2, -2, 0]:
            for c in range(cl_dev):
                hits = [
                    jnp.where((offset_ref[i] == o) & (column_ref[i] == c), 1.0, 0.0).astype(jnp.float32)
                    for i in range(cl_dev * near_cl)
                ]
                target = image.at[c] if o == 0 else returned.at[o + REACH, c]

                def fold(t):
                    rows = pl.ds(pl.multiple_of(t * 64, 64), 64)
                    total = mirrored[0, rows] * hits[0]
                    for i in range(1, cl_dev * near_cl):
                        total = total + mirrored[i, rows] * hits[i]
                    target[rows] = total

                times(panels // 64, fold)
            if o:
                @pl.when(inside(o))
                def _():
                    mirror_copy(o).start()

        if first:
            loads[2].wait()
        for c in range(cl_dev):
            both = fast_dot(own[c], window[REACH, c]) + fast_dot(turned[c], own[c]).T
            image[c] += 0.5 * both + diag_ref[c] * direction[c]

        when_inside(lambda o: window_from(o).wait_recv())

        def forward(i):
            c, q = i // near_cl, i % near_cl
            columns = pl.ds(pl.multiple_of(q * panels, panels), panels)
            image[c] += fast_dot(near[c, :, columns], window[offset_ref[i] + REACH, column_ref[i]])

        times(cl_dev * near_cl, forward)

        times(devices - 1, lambda k: far_copy(k + 1, me, lax.rem(me - k - 1 + devices, devices)).wait_recv())

        def match(i):
            for j in range(8):
                h = i * 8 + j
                matched[h] = incoming[peer_ref[h], rank_ref[h]]

        times(far_dev // 8, match)

        def expand(i):
            c, q = i // tiles, i % tiles
            columns = pl.ds(pl.multiple_of(q * panels, panels), panels)
            value = matched[pl.ds(i * tile_halves, tile_halves)].reshape(panels, modes)
            image[c] += fast_dot(far[c, :, columns], value)

        times(cl_dev * tiles, expand)

        def collect(o):
            mirror_from(o).wait_recv()
            image[...] += landed[REACH + o]

        when_inside(collect)

    def settle():
        when_inside(lambda o: window_copy(o).wait_send())
        when_inside(lambda o: mirror_copy(o).wait_send())
        times(devices - 1, lambda k: far_copy(k + 1, lax.rem(me + k + 1, devices), me).wait_send())

    def flat(ref):
        return ref[...].reshape(cl_dev * panels, modes)

    def combine(ref, coeff):
        return hdot(flat(ref), coeff).reshape(cl_dev, panels, modes)

    def gram(left, right):
        return hdot(flat(left).T, flat(right))

    operate(True)
    grams = jnp.concatenate([gram(direction, direction), gram(direction, image), gram(image, image)], axis=0)
    part_a[...] = grams.reshape(part_a.shape)
    reduce_all(devices, part_a, landing_a, total_a, sems)
    whole = total_a[...].reshape(-1, modes)
    current, curvature, squared = whole[:modes], whole[modes : 2 * modes], whole[2 * modes :]
    inv_curv, inv_cur = invert([symmetric(curvature), symmetric(current)])
    step = hdot(inv_curv, current)
    cross = hdot(curvature, step)
    later = current - cross - cross.T + hdot(step.T, hdot(squared, step))
    blend = hdot(inv_cur, later)
    field_ref[...] = combine(direction, step)
    resid_ref[...] = resid_ref[...] - combine(image, step)
    direction[...] = resid_ref[...] + combine(direction, blend)
    settle()

    operate(False)
    part_b[...] = gram(direction, image).reshape(part_b.shape)
    reduce_all(devices, part_b, landing_b, total_b, sems)
    (inv_curv,) = invert([symmetric(total_b[...].reshape(modes, modes))])
    step = hdot(inv_curv, later)
    field_ref[...] = field_ref[...] + combine(direction, step)
    resid_ref[...] = resid_ref[...] - combine(image, step)
    settle()


def shards(
    right_side, diag_shift, self_blocks, near_blocks, near_offset, near_column, far_factors, far_peer
):
    cl_dev, panels, modes = right_side.shape
    devices = lax.axis_size("clusters")
    far_dev = far_peer.shape[0]
    near_cl = near_blocks.shape[2] // panels
    capacity = max(2, -(-far_dev // devices))
    peers = far_peer[:, 0]
    hot = (peers[:, None] == jnp.arange(devices, dtype=jnp.int32)[None, :]).astype(jnp.int32)
    rank = jnp.sum((jnp.cumsum(hot, axis=0) - hot) * hot, axis=1)
    slot = (peers * capacity + rank)[None, :] == jnp.arange(devices * capacity, dtype=jnp.int32)[:, None]
    halves = jnp.arange(far_dev, dtype=jnp.int32)[None, :]
    source = far_dev + jnp.sum(jnp.where(slot, halves - far_dev, 0), axis=1)
    diag = jnp.broadcast_to(diag_shift[:, :, None], right_side.shape)
    span = 2 * REACH + 1
    block = (cl_dev, panels, modes)
    shape_a = (min(devices, 3 * modes // 8), 3 * modes // min(devices, 3 * modes // 8), modes)
    shape_b = (min(devices, modes // 8), modes // min(devices, modes // 8), modes)
    half = (RANK, modes)
    f32, bf16, dma = jnp.float32, jnp.bfloat16, pltpu.SemaphoreType.DMA
    vmem = pl.BlockSpec(memory_space=pltpu.VMEM)
    smem = pl.BlockSpec(memory_space=pltpu.SMEM)
    anywhere = pl.BlockSpec(memory_space=pl.ANY)
    macs = 2 * 2 * cl_dev * panels * modes * 2 * (panels + near_blocks.shape[2] + far_factors.shape[2])
    return pl.pallas_call(
        functools.partial(kernel, devices),
        out_shape=[jax.ShapeDtypeStruct(block, f32)] * 2,
        in_specs=[vmem] * 2 + [anywhere] * 3 + [smem] * 5,
        out_specs=[vmem] * 2,
        scratch_shapes=[
            pltpu.VMEM(self_blocks.shape, bf16),
            pltpu.VMEM(near_blocks.shape, bf16),
            pltpu.VMEM(far_factors.shape, bf16),
            pltpu.VMEM(block, f32),
            pltpu.VMEM(block, f32),
            pltpu.VMEM((cl_dev, modes, panels), bf16),
            pltpu.VMEM((span,) + block, bf16),
            dma((2, span)),
            pltpu.VMEM((cl_dev * near_cl, panels, modes), f32),
            pltpu.VMEM((span,) + block, f32),
            pltpu.VMEM((span,) + block, f32),
            dma((2, span)),
            pltpu.VMEM((far_dev + 1,) + half, bf16),
            pltpu.VMEM((devices, capacity) + half, bf16),
            pltpu.VMEM((devices, capacity) + half, bf16),
            dma((devices,)),
            dma((devices,)),
            pltpu.VMEM((far_dev,) + half, bf16),
            pltpu.VMEM(shape_a, f32),
            pltpu.VMEM((devices,) + shape_a[1:], f32),
            pltpu.VMEM(shape_a, f32),
            pltpu.VMEM(shape_b, f32),
            pltpu.VMEM((devices,) + shape_b[1:], f32),
            pltpu.VMEM(shape_b, f32),
            dma((3,)),
        ] + [dma((devices,))] * 4,
        compiler_params=pltpu.CompilerParams(collective_id=1, has_side_effects=True, vmem_limit_bytes=48 << 20),
        cost_estimate=pl.CostEstimate(flops=2 * macs, bytes_accessed=12 << 20, transcendentals=0),
    )(right_side, diag, self_blocks, near_blocks, far_factors, near_offset, near_column, peers, rank, source)


def solution(mesh):
    in_specs = (
        P(("groups", "clusters"), None, None),
        P(("groups", "clusters"), None),
        P(("groups", "clusters"), None, None),
        P(("groups", "clusters"), None, None),
        P(("groups", "clusters")),
        P(("groups", "clusters")),
        P(("groups", "clusters"), None, None),
        P(("groups", "clusters"), None),
    )
    out_specs = (P(("groups", "clusters"), None, None), P(("groups", "clusters"), None, None))
    return jax.shard_map(shards, mesh=mesh, in_specs=in_specs, out_specs=out_specs, check_vma=False)
```

```python
import functools

import jax
import jax.numpy as jnp
from jax import lax
from jax.experimental import pallas as pl
from jax.experimental.pallas import tpu as pltpu
from jax.sharding import PartitionSpec as P

MESH = pl.DeviceIdType.MESH
RANK = 32
REACH = 2
STEPS = 32000.0
HIGH = lax.Precision.HIGHEST


def hdot(left, right, dims=((1,), (0,))):
    return lax.dot_general(left, right, (dims, ((), ())), precision=HIGH, preferred_element_type=jnp.float32)


def invert(mats):
    size = mats[0].shape[0]
    rows = lax.broadcasted_iota(jnp.int32, (size, size), 0)
    lanes = lax.broadcasted_iota(jnp.int32, (size, size), 1)

    def body(_, mats):
        done = []
        for a in mats:
            for k in range(8):
                column = a[:, k : k + 1]
                pivot = 1.0 / a[k : k + 1, k : k + 1]
                line = jnp.where(lanes[:1] == k, pivot, a[k : k + 1] * pivot)
                a = jnp.where(rows == k, line, jnp.where(lanes == k, 0.0, a) - column * line)
            a = pltpu.roll(a, size - 8, 1)
            done.append(jnp.concatenate([a[8:], a[:8]], axis=0))
        return tuple(done)

    return lax.fori_loop(0, size // 8, body, tuple(mats))


def meet(devices):
    me = lax.axis_index("clusters")
    barrier = pltpu.get_barrier_semaphore()

    def greet(k, carry):
        peer = lax.rem(me + k, devices)
        pl.semaphore_signal(barrier, inc=1, device_id={"clusters": peer}, device_id_type=MESH)
        return carry

    lax.fori_loop(1, devices, greet, 0)
    pl.semaphore_wait(barrier, devices - 1)


def reduce_all(devices, part, landing, total, sems):
    me = lax.axis_index("clusters")
    pieces = part.shape[0]
    send_a, recv_a, send_b, recv_b = sems

    def copy_a(k, peer):
        return pltpu.make_async_remote_copy(
            src_ref=part.at[peer], dst_ref=landing.at[k], send_sem=send_a.at[k], recv_sem=recv_a.at[k],
            device_id={"clusters": peer}, device_id_type=MESH)

    def copy_b(k, peer, piece):
        return pltpu.make_async_remote_copy(
            src_ref=total.at[piece], dst_ref=total.at[piece], send_sem=send_b.at[k], recv_sem=recv_b.at[k],
            device_id={"clusters": peer}, device_id_type=MESH)

    def loop(fn):
        def body(k, carry):
            fn(k)
            return carry
        lax.fori_loop(1, devices, body, 0)

    def send_one(k):
        peer = lax.rem(me + k, devices)
        if pieces == devices:
            copy_a(k, peer).start()
        else:
            @pl.when(peer < pieces)
            def _():
                copy_a(k, peer).start()

    loop(send_one)

    def gather():
        def add(k, acc):
            copy_a(k, 0).wait_recv()
            return acc + landing[k]
        total[me] = lax.fori_loop(1, devices, add, part[me])
        loop(lambda k: copy_b(k, lax.rem(me + k, devices), me).start())

    if pieces == devices:
        gather()
    else:
        pl.when(me < pieces)(gather)

    def arrive(k):
        origin = lax.rem(me - k + devices, devices)
        if pieces == devices:
            copy_b(k, 0, origin).wait_recv()
        else:
            @pl.when(origin < pieces)
            def _():
                copy_b(k, 0, origin).wait_recv()

    loop(arrive)

    def finish(k):
        peer = lax.rem(me + k, devices)
        if pieces == devices:
            copy_a(k, peer).wait_send()
            copy_b(k, peer, me).wait_send()
        else:
            @pl.when(peer < pieces)
            def _():
                copy_a(k, peer).wait_send()

            @pl.when(me < pieces)
            def _():
                copy_b(k, peer, me).wait_send()

    loop(finish)


def symmetric(mat):
    return 0.5 * (mat + mat.T)


def fast_dot(left, right):
    return jnp.dot(left, right, preferred_element_type=jnp.float32)


def times(count, fn):
    def body(k, carry):
        fn(k)
        return carry
    lax.fori_loop(0, count, body, 0)


def kernel(
    devices, right_ref, diag_ref, self_hbm, near_hbm, far_hbm, offset_ref, column_ref, peer_ref, rank_ref, source_ref,
    field_ref, resid_ref,
    own, near, far, direction, image, turned, window, window_sems, mirrored, returned, landed, scale_out, scale_in, stage, partial, partner, mirror_sems,
    compressed, outgoing, incoming, far_send, far_recv, matched, part_a, landing_a, total_a, part_b, landing_b, total_b,
    load_sems, send_a, recv_a, send_b, recv_b,
):
    me = lax.axis_index("clusters")
    cl_dev, panels, modes = right_ref.shape
    near_cl = near.shape[2] // panels
    far_cl = far.shape[2] // RANK
    capacity = outgoing.shape[1]
    far_dev = cl_dev * far_cl
    offsets = [o for o in range(-REACH, REACH + 1) if o]
    sems = (send_a, recv_a, send_b, recv_b)
    odd = lax.rem(me, 2)
    beside, across, joint = 1 - 2 * odd, 4 * odd - 2, 2 * odd - 1

    loads = [
        pltpu.make_async_copy(far_hbm, far, load_sems.at[0]),
        pltpu.make_async_copy(near_hbm, near, load_sems.at[1]),
        pltpu.make_async_copy(self_hbm, own, load_sems.at[2]),
    ]
    for load in loads:
        load.start()

    def inside(offset):
        return (me + offset >= 0) & (me + offset < devices)

    for offset in offsets:
        @pl.when(jnp.logical_not(inside(offset)))
        def _():
            window[offset + REACH] = jnp.zeros(window.shape[1:], window.dtype)
    compressed[far_dev] = jnp.zeros(compressed.shape[1:], compressed.dtype)
    direction[...] = right_ref[...]
    resid_ref[...] = right_ref[...]
    meet(devices)

    def window_copy(offset):
        return pltpu.make_async_remote_copy(
            src_ref=window.at[REACH], dst_ref=window.at[REACH - offset],
            send_sem=window_sems.at[0, REACH + offset], recv_sem=window_sems.at[1, REACH - offset],
            device_id={"clusters": me + offset}, device_id_type=MESH)

    def window_from(offset):
        return pltpu.make_async_remote_copy(
            src_ref=window.at[REACH], dst_ref=window.at[REACH + offset],
            send_sem=window_sems.at[0, REACH + offset], recv_sem=window_sems.at[1, REACH + offset],
            device_id={"clusters": me + offset}, device_id_type=MESH)

    def window_relay(side):
        return pltpu.make_async_remote_copy(
            src_ref=window.at[REACH + side], dst_ref=window.at[REACH + 2 * side],
            send_sem=window_sems.at[0, REACH], recv_sem=window_sems.at[1, REACH + 2 * side],
            device_id={"clusters": me - side}, device_id_type=MESH)

    def partial_copy():
        return pltpu.make_async_remote_copy(
            src_ref=partial, dst_ref=partner, send_sem=mirror_sems.at[0, 3], recv_sem=mirror_sems.at[1, 3],
            device_id={"clusters": me + beside}, device_id_type=MESH)

    def mirror_copy(kind):
        return pltpu.make_async_remote_copy(
            src_ref=returned.at[kind], dst_ref=landed.at[kind],
            send_sem=mirror_sems.at[0, kind], recv_sem=mirror_sems.at[1, kind],
            device_id={"clusters": me + (beside, across, joint)[kind]}, device_id_type=MESH)

    def scale_copy(kind):
        return pltpu.make_async_remote_copy(
            src_ref=scale_out.at[kind], dst_ref=scale_in.at[kind],
            send_sem=mirror_sems.at[0, 4 + kind], recv_sem=mirror_sems.at[1, 4 + kind],
            device_id={"clusters": me + (beside, across, joint)[kind]}, device_id_type=MESH)

    def post_mirror(kind):
        mirror_copy(kind).start()
        scale_copy(kind).start()

    def sent_mirror(kind):
        mirror_copy(kind).wait_send()
        scale_copy(kind).wait_send()

    def far_copy(k, peer, slot):
        return pltpu.make_async_remote_copy(
            src_ref=outgoing.at[peer], dst_ref=incoming.at[slot], send_sem=far_send.at[k], recv_sem=far_recv.at[k],
            device_id={"clusters": peer}, device_id_type=MESH)

    def when_inside(fn):
        for offset in offsets:
            @pl.when(inside(offset))
            def _():
                fn(offset)

    def when_sent(fn):
        for offset in offsets:
            own_part = inside(offset)
            if offset == 2:
                own_part = own_part & (odd == 0)
            elif offset == -2:
                own_part = own_part & (odd == 1)

            @pl.when(own_part)
            def _():
                fn(offset)

    def when_relay(fn):
        @pl.when((odd == 0) & inside(-1))
        def _():
            fn(-1)

        @pl.when((odd == 1) & inside(1))
        def _():
            fn(1)

    def operate(first):
        for c in range(cl_dev):
            value = direction[c]
            window[REACH, c] = value.astype(jnp.bfloat16)
            turned[c] = value.T.astype(jnp.bfloat16)
        when_sent(lambda o: window_copy(o).start())

        if first:
            loads[0].wait()
        tiles = far_cl * RANK // panels
        tile_halves = panels // RANK

        def compress(i):
            c, q = i // tiles, i % tiles
            columns = pl.ds(pl.multiple_of(q * panels, panels), panels)
            value = fast_dot(turned[c], far[c, :, columns]).T.astype(jnp.bfloat16)
            compressed[pl.ds(i * tile_halves, tile_halves)] = value.reshape(tile_halves, RANK, modes)

        times(cl_dev * tiles, compress)

        def post(k):
            peer = lax.rem(me + k, devices)
            for r in range(capacity):
                outgoing[peer, r] = compressed[source_ref[peer * capacity + r]]

        def send(k):
            post(k + 1)
            far_copy(k + 1, lax.rem(me + k + 1, devices), me).start()

        times(devices - 1, send)
        for r in range(capacity):
            incoming[me, r] = compressed[source_ref[me * capacity + r]]

        if first:
            loads[1].wait()

        def mirror(i):
            c, q = i // near_cl, i % near_cl
            columns = pl.ds(pl.multiple_of(q * panels, panels), panels)
            mirrored[i] = fast_dot(turned[c], near[c, :, columns]).T

        times(cl_dev * near_cl, mirror)

        def relay(side):
            window_from(side).wait_recv()
            window_relay(side).start()

        when_relay(relay)

        def gather(o, target, kind=None, extra=None):
            for c in range(cl_dev):
                hits = [
                    jnp.where((offset_ref[i] == o) & (column_ref[i] == c), 1.0, 0.0).astype(jnp.float32)
                    for i in range(cl_dev * near_cl)
                ]

                def fold(t, top):
                    rows = pl.ds(pl.multiple_of(t * 64, 64), 64)
                    total = mirrored[0, rows] * hits[0]
                    for i in range(1, cl_dev * near_cl):
                        total = total + mirrored[i, rows] * hits[i]
                    if extra is not None:
                        total = total + extra[c, rows]
                    target[c, rows] = total
                    return jnp.maximum(top, jnp.max(jnp.abs(total).reshape(8, 8, modes), axis=0))

                top = lax.fori_loop(0, panels // 64, fold, jnp.zeros((8, modes), jnp.float32))
                if kind is not None:
                    top = jnp.maximum(jnp.max(top, axis=0, keepdims=True), 1e-30)
                    scale_out[kind, c] = jnp.broadcast_to(top * (1.0 / STEPS), (8, modes))
                    finer = STEPS / top

                    def code(t):
                        rows = pl.ds(pl.multiple_of(t * 64, 64), 64)
                        value = jnp.floor(target[c, rows] * finer + 0.5)
                        returned[kind, c, rows] = value.astype(jnp.int32).astype(jnp.int16)

                    times(panels // 64, code)

        gather(-across, partial)
        partial_copy().start()
        gather(across, stage, 1)

        @pl.when(inside(across))
        def _():
            post_mirror(1)

        gather(beside, stage, 0)
        post_mirror(0)
        partial_copy().wait_recv()
        gather(joint, stage, 2, partner)

        @pl.when(inside(joint))
        def _():
            post_mirror(2)

        gather(0, image)

        if first:
            loads[2].wait()
        for c in range(cl_dev):
            both = fast_dot(own[c], window[REACH, c]) + fast_dot(turned[c], own[c]).T
            image[c] += 0.5 * both + diag_ref[c] * direction[c]

        for side in (-1, 1):
            taken = (odd == 0) if side < 0 else (odd == 1)

            @pl.when(inside(side) & jnp.logical_not(taken))
            def _():
                window_from(side).wait_recv()

            @pl.when(inside(2 * side))
            def _():
                window_from(2 * side).wait_recv()


        def forward(i):
            c, q = i // near_cl, i % near_cl
            columns = pl.ds(pl.multiple_of(q * panels, panels), panels)
            image[c] += fast_dot(near[c, :, columns], window[offset_ref[i] + REACH, column_ref[i]])

        times(cl_dev * near_cl, forward)

        times(devices - 1, lambda k: far_copy(k + 1, me, lax.rem(me - k - 1 + devices, devices)).wait_recv())

        def match(i):
            for j in range(8):
                h = i * 8 + j
                matched[h] = incoming[peer_ref[h], rank_ref[h]]

        times(far_dev // 8, match)

        def expand(i):
            c, q = i // tiles, i % tiles
            columns = pl.ds(pl.multiple_of(q * panels, panels), panels)
            value = matched[pl.ds(i * tile_halves, tile_halves)].reshape(panels, modes)
            image[c] += fast_dot(far[c, :, columns], value)

        times(cl_dev * tiles, expand)

        def collect(kind):
            mirror_copy(kind).wait_recv()
            scale_copy(kind).wait_recv()
            for c in range(cl_dev):
                value = landed[kind, c].astype(jnp.int32).astype(jnp.float32)
                image[c] += value * scale_in[kind, c, 0:1]

        collect(0)
        pl.when(inside(-across))(lambda: collect(1))
        pl.when(inside(joint))(lambda: collect(2))
        when_sent(lambda o: window_copy(o).wait_send())
        when_relay(lambda side: window_relay(side).wait_send())
        partial_copy().wait_send()
        sent_mirror(0)
        pl.when(inside(across))(lambda: sent_mirror(1))
        pl.when(inside(joint))(lambda: sent_mirror(2))
        times(devices - 1, lambda k: far_copy(k + 1, lax.rem(me + k + 1, devices), me).wait_send())

    def flat(ref):
        return ref[...].reshape(cl_dev * panels, modes)

    def combine(ref, coeff):
        return hdot(flat(ref), coeff).reshape(cl_dev, panels, modes)

    def gram(left, right):
        return hdot(flat(left).T, flat(right))

    operate(True)
    grams = jnp.concatenate([gram(direction, direction), gram(direction, image), gram(image, image)], axis=0)
    part_a[...] = grams.reshape(part_a.shape)
    reduce_all(devices, part_a, landing_a, total_a, sems)
    whole = total_a[...].reshape(-1, modes)
    current, curvature, squared = whole[:modes], whole[modes : 2 * modes], whole[2 * modes :]
    inv_curv, inv_cur = invert([symmetric(curvature), symmetric(current)])
    step = hdot(inv_curv, current)
    cross = hdot(curvature, step)
    later = current - cross - cross.T + hdot(step.T, hdot(squared, step))
    blend = hdot(inv_cur, later)
    field_ref[...] = combine(direction, step)
    resid_ref[...] = resid_ref[...] - combine(image, step)
    direction[...] = resid_ref[...] + combine(direction, blend)

    operate(False)
    part_b[...] = gram(direction, image).reshape(part_b.shape)
    reduce_all(devices, part_b, landing_b, total_b, sems)
    (inv_curv,) = invert([symmetric(total_b[...].reshape(modes, modes))])
    step = hdot(inv_curv, later)
    field_ref[...] = field_ref[...] + combine(direction, step)
    resid_ref[...] = resid_ref[...] - combine(image, step)


def shards(
    right_side, diag_shift, self_blocks, near_blocks, near_offset, near_column, far_factors, far_peer
):
    cl_dev, panels, modes = right_side.shape
    devices = lax.axis_size("clusters")
    far_dev = far_peer.shape[0]
    near_cl = near_blocks.shape[2] // panels
    capacity = max(2, -(-far_dev // devices))
    peers = far_peer[:, 0]
    hot = (peers[:, None] == jnp.arange(devices, dtype=jnp.int32)[None, :]).astype(jnp.int32)
    rank = jnp.sum((jnp.cumsum(hot, axis=0) - hot) * hot, axis=1)
    slot = (peers * capacity + rank)[None, :] == jnp.arange(devices * capacity, dtype=jnp.int32)[:, None]
    halves = jnp.arange(far_dev, dtype=jnp.int32)[None, :]
    source = far_dev + jnp.sum(jnp.where(slot, halves - far_dev, 0), axis=1)
    diag = jnp.broadcast_to(diag_shift[:, :, None], right_side.shape)
    span = 2 * REACH + 1
    block = (cl_dev, panels, modes)
    shape_a = (min(devices, 3 * modes // 8), 3 * modes // min(devices, 3 * modes // 8), modes)
    shape_b = (min(devices, modes // 8), modes // min(devices, modes // 8), modes)
    half = (RANK, modes)
    f32, bf16, dma = jnp.float32, jnp.bfloat16, pltpu.SemaphoreType.DMA
    vmem = pl.BlockSpec(memory_space=pltpu.VMEM)
    smem = pl.BlockSpec(memory_space=pltpu.SMEM)
    anywhere = pl.BlockSpec(memory_space=pl.ANY)
    macs = 2 * 2 * cl_dev * panels * modes * 2 * (panels + near_blocks.shape[2] + far_factors.shape[2])
    return pl.pallas_call(
        functools.partial(kernel, devices),
        out_shape=[jax.ShapeDtypeStruct(block, f32)] * 2,
        in_specs=[vmem] * 2 + [anywhere] * 3 + [smem] * 5,
        out_specs=[vmem] * 2,
        scratch_shapes=[
            pltpu.VMEM(self_blocks.shape, bf16),
            pltpu.VMEM(near_blocks.shape, bf16),
            pltpu.VMEM(far_factors.shape, bf16),
            pltpu.VMEM(block, f32),
            pltpu.VMEM(block, f32),
            pltpu.VMEM((cl_dev, modes, panels), bf16),
            pltpu.VMEM((span,) + block, bf16),
            dma((2, span)),
            pltpu.VMEM((cl_dev * near_cl, panels, modes), f32),
            pltpu.VMEM((3,) + block, jnp.int16),
            pltpu.VMEM((3,) + block, jnp.int16),
            pltpu.VMEM((3, cl_dev, 8, modes), f32),
            pltpu.VMEM((3, cl_dev, 8, modes), f32),
            pltpu.VMEM(block, f32),
            pltpu.VMEM(block, f32),
            pltpu.VMEM(block, f32),
            dma((2, 7)),
            pltpu.VMEM((far_dev + 1,) + half, bf16),
            pltpu.VMEM((devices, capacity) + half, bf16),
            pltpu.VMEM((devices, capacity) + half, bf16),
            dma((devices,)),
            dma((devices,)),
            pltpu.VMEM((far_dev,) + half, bf16),
            pltpu.VMEM(shape_a, f32),
            pltpu.VMEM((devices,) + shape_a[1:], f32),
            pltpu.VMEM(shape_a, f32),
            pltpu.VMEM(shape_b, f32),
            pltpu.VMEM((devices,) + shape_b[1:], f32),
            pltpu.VMEM(shape_b, f32),
            dma((3,)),
        ] + [dma((devices,))] * 4,
        compiler_params=pltpu.CompilerParams(collective_id=1, has_side_effects=True, vmem_limit_bytes=48 << 20),
        cost_estimate=pl.CostEstimate(flops=2 * macs, bytes_accessed=12 << 20, transcendentals=0),
    )(right_side, diag, self_blocks, near_blocks, far_factors, near_offset, near_column, peers, rank, source)


def solution(mesh):
    in_specs = (
        P(("groups", "clusters"), None, None),
        P(("groups", "clusters"), None),
        P(("groups", "clusters"), None, None),
        P(("groups", "clusters"), None, None),
        P(("groups", "clusters")),
        P(("groups", "clusters")),
        P(("groups", "clusters"), None, None),
        P(("groups", "clusters"), None),
    )
    out_specs = (P(("groups", "clusters"), None, None), P(("groups", "clusters"), None, None))
    return jax.shard_map(shards, mesh=mesh, in_specs=in_specs, out_specs=out_specs, check_vma=False)
```
